256 devices in a mesh: expert: 32 (over y, z), fsdp: 8 (over x, core).
Axes of the slice: x: 4, y: 4, z: 8, core: 2. Of those that a mesh axis runs over, the one named last changes fastest.
Arguments:
- tokens: bfloat16 [32768, 1024], P(('expert', 'fsdp')), may hold values from -6 to 6
- routes: int32 [32768, 8], P(('expert', 'fsdp')), may hold values from 0 to 63, all different within a row; in each aligned block of 128 rows (0 to 127, 128 to 255, ...) at most 20 rows name the same one
- gates: float32 [32768, 8], P(('expert', 'fsdp')), may hold values from 0.05 to 1
- w_gate: bfloat16 [64, 1024, 512], P('expert', 'fsdp'), may hold values from -0.1875 to 0.1875
- w_up: bfloat16 [64, 1024, 512], P('expert', 'fsdp'), may hold values from -0.1875 to 0.1875
- w_down: bfloat16 [64, 512, 1024], P('expert', None, 'fsdp'), may hold values from -0.25 to 0.25
- cotangent: bfloat16 [32768, 1024], P(('expert', 'fsdp')), may hold values from -6 to 6
Outputs:
- mixed: bfloat16 [32768, 1024], P(('expert', 'fsdp'))
- token_grad: bfloat16 [32768, 1024], P(('expert', 'fsdp'))
- gate_grad: float32 [32768, 8], P(('expert', 'fsdp'))
- grad_gate: float32 [64, 1024, 512], P('expert', 'fsdp')
- grad_up: float32 [64, 1024, 512], P('expert', 'fsdp')
- grad_down: float32 [64, 512, 1024], P('expert', None, 'fsdp')
The draws below stay inside these ranges and needn't reach their ends.
Inputs may be any that keep to these rules, and one draw needn't show every extreme that they name: `routes`: each row names 8 different experts; among the 128 rows of one device (aligned blocks) no expert is named more than 20 times.
All inputs are finite; a program needn't handle non-finite values.
Results may differ from the reference program's by a relative error of at most 0.015.
Values may be sent and summed in bfloat16 or wider, within the bound.
No kernel may reach another device: no remote copies, remote signals or barrier semaphores. Data moves between devices by JAX's collectives and lax.ppermute only.
A program may use at most 128 MiB of HBM per device.

```python
import math
import jax
import jax.numpy as jnp
import numpy as np
from jax import lax

D = 1024
FF = 512
TOPK = 8
TOK_DEV = 128
EXPERTS = 64
MOST = 20
TOKENS = 32768
N_EXPERT = 32
N_FSDP = 8


def block_levels(stream_key, dims, shards, least, top_value):
    factor_of, own = 1.0, jax.random.fold_in(stream_key, 6)
    for axis_at, blocks in shards:
        draws = jnp.exp(jax.random.uniform(jax.random.fold_in(own, axis_at), (blocks,), jnp.float32, least / len(shards), top_value / len(shards)))
        factor_of = factor_of * jnp.repeat(draws, dims[axis_at] // blocks).reshape([-1 if axis == axis_at else 1 for axis in range(len(dims))])
    return factor_of


def shared_out(rng, own, number, rows, count, top, limit, slope):
    sequence = jax.random.permutation(rng, count)
    heavy_load, usual = shares(count, rows * top, limit, slope, True), shares(count, rows * top, limit, slope, False)
    places = jnp.arange(count)

    def named(tallies, offset_by):
        used = int((tallies > 0).sum())
        fixed = max(1, used // 4)
        shifted = fixed + (places - fixed + offset_by * (used - fixed)) % max(1, count - fixed)
        return jnp.zeros((count,), jnp.int32).at[sequence[jnp.where(places < fixed, places, shifted)]].set(jnp.asarray(tallies, jnp.int32))

    tallies = jnp.where(number % 4 == 0, named(heavy_load, number // 4), named(usual, number - number // 4 - 1))
    mixed = jax.random.permutation(jax.random.fold_in(own, 3), count)
    source_of, taker = mixed[0:count // 2 * 2:2], mixed[1:count // 2 * 2:2]
    room = jnp.minimum(tallies[source_of] - 1, limit - tallies[taker]) // 2
    room = jnp.where((source_of == sequence[0]) | (taker == sequence[0]) | (tallies[taker] == 0), 0, jnp.maximum(room, 0))
    shifted = jax.random.randint(jax.random.fold_in(own, 4), (count // 2,), 0, 1 << 20) % (room + 1)
    tallies = tallies.at[source_of].add(-shifted).at[taker].add(shifted)
    labels = jnp.searchsorted(jnp.cumsum(tallies), jnp.arange(rows * top), side="right").astype(jnp.int32)
    listing = labels.reshape(top, rows).T
    listing = listing[jax.random.permutation(jax.random.fold_in(own, 1), rows)]
    offset_by = jax.random.randint(jax.random.fold_in(own, 2), (rows, 1), 0, top)
    return jnp.take_along_axis(listing, (jnp.arange(top)[None, :] + offset_by) % top, axis=1)


def shares(count, total, reach, slope, full):
    weights = [(1 << 20) // math.isqrt(grade ** slope) + 1 for grade in range(1, count + 1)]
    largest = reach if full else min(reach, max(-(-total // count), total * weights[0] // sum(weights)))
    least = 1 if total - largest >= count - 1 else 0
    holding, spare = [largest] + [least] * (count - 1), total - largest - least * (count - 1)
    while spare > 0:
        candidates = [i for i in range(1, count) if holding[i] < largest] or [i for i in range(1, count) if holding[i] < reach]
        whole, remaining = sum([weights[i] for i in candidates]), spare
        for i in candidates:
            more = min(reach - holding[i], max(1, remaining * weights[i] // whole), spare)
            holding[i] = holding[i] + more
            spare = spare - more
    return np.array(holding)


def noise(stream_key, dims, deviation, bound, split=(), held_as=jnp.bfloat16):
    result = jax.random.normal(stream_key, dims, jnp.float32) * deviation
    if len(split) > 0:
        result = block_levels(stream_key, dims, split, -0.22, 0.18) * result
    return jnp.clip(result, min=-bound, max=bound).astype(held_as)


def setup_inputs(seed: int = 0) -> dict:
    key_of = jax.random.split(jax.random.key(seed), 8)
    tokens = noise(key_of[0], (TOKENS, D), 1.0, 6.0, ((0, 256),))
    routes_keys = jax.random.split(jax.random.fold_in(key_of[1], 1), TOKENS // TOK_DEV)
    routes_turns = jax.random.permutation(jax.random.fold_in(key_of[1], 3), TOKENS // TOK_DEV)
    routes = jax.vmap(lambda own, number: shared_out(jax.random.fold_in(key_of[1], 2), own, number, TOK_DEV, EXPERTS, TOPK, MOST, 2))(routes_keys, routes_turns).reshape((TOKENS, TOPK))
    gates = jnp.clip(jnp.exp(math.log(1.0) - 2.9957323 * jax.random.uniform(key_of[2], (TOKENS, TOPK), jnp.float32) ** block_levels(key_of[2], (TOKENS, TOPK), ((0, 256),), -0.2, 0.2)), 0.05, 1.0)
    w_gate = noise(key_of[3], (EXPERTS, D, FF), D ** -0.5, 0.1875, ((0, 32), (1, 8)))
    w_up = noise(key_of[4], (EXPERTS, D, FF), D ** -0.5, 0.1875, ((0, 32), (1, 8)))
    w_down = noise(key_of[5], (EXPERTS, FF, D), FF ** -0.5, 0.25, ((0, 32), (2, 8)))
    cotangent = noise(key_of[6], (TOKENS, D), 1.0, 6.0, ((0, 256),))
    return {"tokens": tokens, "routes": routes, "gates": gates, "w_gate": w_gate, "w_up": w_up, "w_down": w_down, "cotangent": cotangent}


def expert_pass(x_rows, s_rows, wg, wu, wd):
    gate_pre = jnp.dot(x_rows, wg, preferred_element_type=jnp.float32)
    up_pre = jnp.dot(x_rows, wu, preferred_element_type=jnp.float32)
    sigmoid_gate = jax.nn.sigmoid(gate_pre)
    activated = gate_pre * sigmoid_gate
    hidden = (activated * up_pre).astype(jnp.bfloat16)
    out_rows = jnp.dot(hidden, wd, preferred_element_type=jnp.float32).astype(jnp.bfloat16)
    hidden_grad = jnp.dot(s_rows, wd.T, preferred_element_type=jnp.float32)
    gate_pre_grad = (hidden_grad * up_pre * sigmoid_gate * (1.0 + gate_pre * (1.0 - sigmoid_gate))).astype(jnp.bfloat16)
    up_pre_grad = (hidden_grad * activated).astype(jnp.bfloat16)
    pair_grad = (jnp.dot(gate_pre_grad, wg.T, preferred_element_type=jnp.float32)
                 + jnp.dot(up_pre_grad, wu.T, preferred_element_type=jnp.float32)).astype(jnp.bfloat16)
    part_gate = jnp.dot(x_rows.T, gate_pre_grad, preferred_element_type=jnp.float32).astype(jnp.bfloat16)
    part_up = jnp.dot(x_rows.T, up_pre_grad, preferred_element_type=jnp.float32).astype(jnp.bfloat16)
    part_down = jnp.dot(hidden.T, s_rows, preferred_element_type=jnp.float32).astype(jnp.bfloat16)
    return out_rows, pair_grad, part_gate, part_up, part_down


def regroup(array):
    tail = array.shape[1:]
    shaped = array.reshape((N_EXPERT, N_FSDP, TOK_DEV) + tail)
    shaped = jnp.swapaxes(shaped, 0, 1)
    return shaped.reshape((N_FSDP, N_EXPERT * TOK_DEV) + tail)


def ungroup(array):
    tail = array.shape[2:]
    shaped = array.reshape((N_FSDP, N_EXPERT, TOK_DEV) + tail)
    shaped = jnp.swapaxes(shaped, 0, 1)
    return shaped.reshape((TOKENS,) + tail)


def reference(tokens, routes, gates, w_gate, w_up, w_down, cotangent):
    group_tokens = N_EXPERT * TOK_DEV
    pair_count = group_tokens * TOPK
    span = N_EXPERT * MOST
    model_width = tokens.shape[1]

    def group_pass(totals, inputs):
        x_group, r_group, g_group, dy_group = inputs
        flat_routes = r_group.reshape(-1).astype(jnp.int32)
        order = jnp.argsort(flat_routes, stable=True).astype(jnp.int32)
        onehot = flat_routes[:, None] == jnp.arange(EXPERTS, dtype=jnp.int32)[None, :]
        counts = jnp.sum(onehot.astype(jnp.int32), axis=0).astype(jnp.int32)
        offsets = (jnp.cumsum(counts) - counts).astype(jnp.int32)
        scaled = (g_group[:, :, None] * dy_group[:, None, :].astype(jnp.float32)).astype(jnp.bfloat16)
        scaled = scaled.reshape(pair_count, model_width)

        def per_expert(expert_id):
            position = jnp.arange(span, dtype=jnp.int32)
            valid = position < counts[expert_id]
            pair = order[jnp.minimum(offsets[expert_id] + position, pair_count - 1)]
            x_rows = jnp.where(valid[:, None], x_group[pair // TOPK], jnp.zeros((), jnp.bfloat16))
            s_rows = jnp.where(valid[:, None], scaled[pair], jnp.zeros((), jnp.bfloat16))
            results = expert_pass(x_rows, s_rows, w_gate[expert_id], w_up[expert_id], w_down[expert_id])
            target = jnp.where(valid, pair, pair_count).astype(jnp.int32)
            return results + (target,)

        out_rows, pair_rows, part_gate, part_up, part_down, target = lax.map(
            per_expert, jnp.arange(EXPERTS, dtype=jnp.int32))
        target = target.reshape(-1)
        out_pairs = jnp.zeros((pair_count, model_width), jnp.bfloat16).at[target].set(
            out_rows.reshape(-1, model_width), mode="drop")
        grad_pairs = jnp.zeros((pair_count, model_width), jnp.bfloat16).at[target].set(
            pair_rows.reshape(-1, model_width), mode="drop")
        out_pairs = out_pairs.reshape(group_tokens, TOPK, model_width).astype(jnp.float32)
        mixed = jnp.einsum('tk,tkd->td', g_group, out_pairs).astype(jnp.bfloat16)
        gate_grad = jnp.einsum('td,tkd->tk', dy_group.astype(jnp.float32), out_pairs)
        token_grad = jnp.sum(grad_pairs.reshape(group_tokens, TOPK, model_width).astype(jnp.float32), axis=1).astype(jnp.bfloat16)
        part_gate = lax.optimization_barrier(part_gate)
        part_up = lax.optimization_barrier(part_up)
        part_down = lax.optimization_barrier(part_down)
        totals = (totals[0] + part_gate.astype(jnp.float32),
                  totals[1] + part_up.astype(jnp.float32),
                  totals[2] + part_down.astype(jnp.float32))
        return totals, (mixed, token_grad, gate_grad)

    start_totals = (jnp.zeros(w_gate.shape, jnp.float32), jnp.zeros(w_up.shape, jnp.float32),
                    jnp.zeros(w_down.shape, jnp.float32))
    totals, stacked = lax.scan(group_pass, start_totals,
                               (regroup(tokens), regroup(routes), regroup(gates), regroup(cotangent)))
    mixed = ungroup(stacked[0])
    token_grad = ungroup(stacked[1])
    gate_grad = ungroup(stacked[2])
    return mixed, token_grad, gate_grad, totals[0], totals[1], totals[2]
```

```python
import jax
import jax.numpy as jnp
from jax import lax
from jax.experimental import pallas as pl
from jax.experimental.pallas import tpu as pltpu
from jax.sharding import PartitionSpec as P

NY, NZ, NF = 4, 8, 8
LOCAL = 2
D, FF, TOPK, TOK = 1024, 512, 8, 128
CAP = 20
META = 128
BF, F32 = jnp.bfloat16, jnp.float32
LIMIT = 56 * 1024 * 1024

GROUPS = ((0,), (1, -1), (2, -2), (3, -3), (4,))


def rows_of(group):
    return -(-len(group) * CAP // 8) * 8


def nn(a, b):
    return lax.dot_general(a, b, (((1,), (0,)), ((), ())), preferred_element_type=F32)


def nt(a, b):
    return lax.dot_general(a, b, (((1,), (1,)), ((), ())), preferred_element_type=F32)


def tn(a, b):
    return lax.dot_general(a, b, (((0,), (0,)), ((), ())), preferred_element_type=F32)


def split3(v):
    hi = v.astype(BF)
    rest = v - hi.astype(F32)
    mid = rest.astype(BF)
    low = (rest - mid.astype(F32)).astype(BF)
    return [hi, mid, low]


def join3(block):
    return (block[0:8] + block[8:16]) + block[16:24]


def prep_kernel(tok_ref, routes_ref, gates_ref, out_ref):
    out_ref[:, 0:D] = tok_ref[...]
    parts = [routes_ref[...].astype(F32)] + [p.astype(F32) for p in split3(gates_ref[...])]
    parts.append(jnp.zeros((TOK - 32, META), F32))
    out_ref[:, D:] = jnp.concatenate(parts, axis=0).astype(BF)


def selection(ids, metas, depth):
    lanes = TOK * len(metas)
    blocks = [m.astype(F32) for m in metas]
    routes = jnp.concatenate([b[0:8] for b in blocks], axis=1)
    gates = jnp.concatenate([join3(b[8:32]) for b in blocks], axis=1)
    hits = [routes[k : k + 1, :] == ids for k in range(TOPK)]
    mask = jnp.zeros((8, lanes), F32)
    gate = jnp.zeros((8, lanes), F32)
    for k in range(TOPK):
        mask = mask + jnp.where(hits[k], 1.0, 0.0)
        gate = gate + jnp.where(hits[k], gates[k : k + 1, :], 0.0)
    above = lax.broadcasted_iota(jnp.int32, (lanes, lanes), 0)
    along = lax.broadcasted_iota(jnp.int32, (lanes, lanes), 1)
    earlier = (above < along) & (above // TOK == along // TOK)
    rank = nn(mask.astype(BF), jnp.where(earlier, 1.0, 0.0).astype(BF))
    chunk = lax.broadcasted_iota(jnp.int32, (8, lanes), 1) // TOK
    key = jnp.where(mask > 0.5, rank.astype(jnp.int32) + CAP * chunk, -1)
    place = lax.broadcasted_iota(jnp.int32, (8, depth, lanes), 1)
    pick = jnp.where(key[:, None, :] == place, 1.0, 0.0)
    row_gate = jnp.sum(pick * gate[:, None, :], axis=2, keepdims=True)
    return pick, row_gate, hits


def pack_kernel(group, *refs):
    count, depth = len(group), rows_of(group)
    ids_ref, refs = refs[0], refs[1:]
    toks, cots, outs = refs[:count], refs[count : 2 * count], refs[2 * count :]
    pick, row_gate, _ = selection(ids_ref[:, 0:1], [r[0:32, D:] for r in toks], depth)
    flat = pick.reshape(8 * depth, TOK * count).astype(BF)
    rows = nn(flat, jnp.concatenate([r[:, 0:D] for r in toks], axis=0)).reshape(8, depth, D)
    grads = nn(flat, jnp.concatenate([r[...] for r in cots], axis=0)).reshape(8, depth, D)
    grads = grads * row_gate
    for r in range(NY):
        outs[r][:, :, 0:D] = rows[2 * r : 2 * r + 2].astype(BF)
        outs[r][:, :, D:] = grads[2 * r : 2 * r + 2].astype(BF)


def expert_kernel(depth, *refs):
    ins, w_ref = refs[:NY], refs[NY]
    outs = refs[NY + 1 : 2 * NY + 1]
    rows_ref, hid_ref, gg_ref, ug_ref, stage = refs[2 * NY + 1 :]
    for r in range(NY):
        stage[r * depth : (r + 1) * depth, :] = ins[r][0].astype(F32)
    rows_ref[0] = stage[...].astype(BF)
    feats, grads = rows_ref[0, :, 0:D], rows_ref[0, :, D:]
    w_gate = w_ref[:, 0, 0].reshape(D, FF)
    w_up = w_ref[:, 1, 0].reshape(D, FF)
    w_down = w_ref[:, 2, 0].reshape(D, FF)
    gate_pre = nn(feats, w_gate)
    up_pre = nn(feats, w_up)
    sig = jax.nn.sigmoid(gate_pre)
    act = gate_pre * sig
    hidden = (act * up_pre).astype(BF)
    out = nt(hidden, w_down)
    for r in range(NY):
        outs[r][0, :, 0:D] = out[r * depth : (r + 1) * depth].astype(BF)
    hidden_grad = nn(grads, w_down)
    gate_grad = (hidden_grad * up_pre * sig * (1.0 + gate_pre * (1.0 - sig))).astype(BF)
    up_grad = (hidden_grad * act).astype(BF)
    back = nt(gate_grad, w_gate) + nt(up_grad, w_up)
    for r in range(NY):
        outs[r][0, :, D:] = back[r * depth : (r + 1) * depth].astype(BF)
    hid_ref[0], gg_ref[0], ug_ref[0] = hidden, gate_grad, up_grad


def weight_kernel(*refs):
    out_ref, refs = refs[-1], refs[:-1]
    held = [jnp.concatenate([r[0] for r in refs[i::4]], axis=0) for i in range(4)]
    rows, hid, gate, up = held
    feats, grads = rows[:, 0:D], rows[:, D:]
    for i, (a, b) in enumerate(((feats, gate), (feats, up), (grads, hid))):
        out_ref[:, i, 0] = tn(a, b).astype(BF).reshape(NF, D // NF, FF)


def combine_kernel(group, taken, *refs):
    count, depth = len(group), rows_of(group)
    lanes = TOK * count
    refs = list(refs)

    def take(n):
        head = refs[:n]
        del refs[:n]
        return head

    (ids_ref,) = take(1)
    toks, cots, backs = take(count), take(count), take(NY)
    sums = [(take(a), take(b)) for a, b in taken]
    pick, row_gate, hits = selection(ids_ref[:, 0:1], [r[0:32, D:] for r in toks], depth)
    flat = pick.reshape(8 * depth, lanes).astype(BF)
    out = jnp.concatenate([r[:, :, 0:D].astype(F32) for r in backs], axis=0)
    back = jnp.concatenate([r[:, :, D:].astype(F32) for r in backs], axis=0)
    cot = nn(flat, jnp.concatenate([r[...] for r in cots], axis=0)).reshape(8, depth, D)
    dots = jnp.sum(cot * out, axis=2, keepdims=True)
    by_expert = jnp.sum(pick * dots, axis=1)
    gate_grad = jnp.concatenate(
        [jnp.sum(jnp.where(h, by_expert, 0.0), axis=0, keepdims=True) for h in hits], axis=0
    )
    mixed = tn(flat, (out * row_gate).reshape(8 * depth, D).astype(BF))
    token = tn(flat, back.reshape(8 * depth, D).astype(BF))
    for i in range(count):
        mix, tok = mixed[i * TOK : (i + 1) * TOK], token[i * TOK : (i + 1) * TOK]
        ggt = gate_grad[:, i * TOK : (i + 1) * TOK]
        for s in sums[i][0]:
            mix = mix + s[...].astype(F32)
        for s in sums[i][1]:
            tok = tok + s[:, 0:D].astype(F32)
            ggt = ggt + join3(s[0:32, D:].astype(F32))
        if group == (0,):
            mix_ref, tok_ref, gg_ref = take(3)
            gg_ref[...] = ggt
        else:
            mix_ref, tok_ref = take(2)
            parts = [p.astype(F32) for p in split3(ggt)] + [jnp.zeros((TOK - 24, META), F32)]
            tok_ref[:, D:] = jnp.concatenate(parts, axis=0).astype(BF)
        mix_ref[...] = mix.astype(BF)
        tok_ref[:, 0:D] = tok.astype(BF)


def shape(*dims, dtype=BF):
    return jax.ShapeDtypeStruct(dims, dtype)


def params(**kw):
    return pltpu.CompilerParams(vmem_limit_bytes=LIMIT, **kw)


def cost(flops, nbytes):
    return pl.CostEstimate(flops=int(flops), bytes_accessed=int(nbytes), transcendentals=0)


def along_z(a, step):
    pairs = [(y * NZ + z, y * NZ + (z + step) % NZ) for y in range(NY) for z in range(NZ)]
    return lax.ppermute(a, "expert", pairs)


def along_y(a, step):
    if step % NY == 0:
        return a
    pairs = [(y * NZ + z, (y + step) % NY * NZ + z) for y in range(NY) for z in range(NZ)]
    return lax.ppermute(a, "expert", pairs)


def body(tokens, routes, gates, w_gate, w_up, w_down, cotangent):
    spot = lax.axis_index("expert")
    at_y, at_z = spot // NZ, spot % NZ
    own = jnp.arange(2 * NY, dtype=jnp.int32)
    ids = LOCAL * ((at_y + own // 2) % NY * NZ + at_z) + own % 2
    ids = jnp.broadcast_to(ids.astype(F32)[:, None], (8, 128))

    shards = jnp.stack([w_gate, w_up, jnp.swapaxes(w_down, 1, 2)], axis=0)
    weights = lax.all_gather(shards, "fsdp", axis=0, tiled=False)

    toks, cots = {}, {}
    toks[0] = pl.pallas_call(prep_kernel, out_shape=shape(TOK, D + META), name="prep")(
        tokens, routes.T, gates.T
    )
    cots[0] = cotangent
    for d in range(1, 5):
        for sign in (1, -1):
            if d < 4 or sign == 1:
                toks[sign * d] = along_z(toks[sign * (d - 1)], sign)
            if d < 4:
                cots[sign * d] = along_z(cots[sign * (d - 1)], sign)
    cots[4] = along_z(cots[-3], -1)

    arrived = {}
    for group in GROUPS:
        depth = rows_of(group)
        packed = pl.pallas_call(
            lambda *refs, group=group: pack_kernel(group, *refs),
            out_shape=[shape(2, depth, 2 * D)] * NY,
            name="pack",
            compiler_params=params(),
            cost_estimate=cost(2 * 8 * depth * TOK * len(group) * 2 * D, 4 << 20),
        )(ids, *[toks[c] for c in group], *[cots[c] for c in group])
        arrived[group] = [along_y(packed[r], r) for r in range(NY)]

    kept, returned = {}, {}
    for group in GROUPS:
        depth = rows_of(group)
        rows = NY * depth
        block = pl.BlockSpec((1, depth, 2 * D), lambda j: (j, 0, 0))
        wide = pl.BlockSpec((1, rows, 2 * D), lambda j: (j, 0, 0))
        narrow = pl.BlockSpec((1, rows, FF), lambda j: (j, 0, 0))
        made = pl.pallas_call(
            lambda *refs, depth=depth: expert_kernel(depth, *refs),
            grid=(LOCAL,),
            in_specs=[block] * NY
            + [pl.BlockSpec((NF, 3, 1, D // NF, FF), lambda j: (0, 0, j, 0, 0))],
            out_specs=[block] * NY + [wide] + [narrow] * 3,
            out_shape=[shape(2, depth, 2 * D)] * NY
            + [shape(2, rows, 2 * D)]
            + [shape(2, rows, FF)] * 3,
            scratch_shapes=[pltpu.VMEM((rows, 2 * D), F32)],
            name="expert",
            compiler_params=params(),
            cost_estimate=cost(2 * 2 * rows * 6 * D * FF, 10 << 20),
        )(*arrived[group], weights)
        returned[group] = made[:NY]
        kept[group] = made[NY:]

    back = {g: [along_y(returned[g][r], -r) for r in range(NY)] for g in GROUPS[::-1]}

    saved = [a for g in GROUPS for a in kept[g]]
    partial = pl.pallas_call(
        weight_kernel,
        grid=(LOCAL,),
        in_specs=[pl.BlockSpec((1,) + a.shape[1:], lambda j: (j, 0, 0)) for a in saved],
        out_specs=pl.BlockSpec((NF, 3, 1, D // NF, FF), lambda j: (0, 0, j, 0, 0)),
        out_shape=shape(NF, 3, LOCAL, D // NF, FF),
        name="weight_grads",
        compiler_params=params(),
        cost_estimate=cost(2 * 2 * 672 * 3 * D * FF, 16 << 20),
    )(*saved)
    summed = lax.psum_scatter(partial, "fsdp", scatter_dimension=0, tiled=False)

    mixes, grads = {}, {}
    for group in GROUPS[::-1]:
        depth = rows_of(group)
        sums = []
        for c in group:
            sources = (1, -1) if c == 0 else (c // abs(c),)
            sums.append(
                (
                    [mixes[s] for s in sources if s in mixes],
                    [grads[s] for s in sources if s in grads],
                )
            )
        last = group == (0,)
        shapes = [shape(TOK, D), shape(TOK, D if last else D + META)] * len(group)
        if last:
            shapes.append(shape(TOPK, TOK, dtype=F32))
        made = pl.pallas_call(
            lambda *refs, group=group, taken=[(len(a), len(b)) for a, b in sums]: combine_kernel(
                group, taken, *refs
            ),
            out_shape=shapes,
            name="combine",
            compiler_params=params(),
            cost_estimate=cost(2 * 8 * depth * TOK * len(group) * 3 * D, 6 << 20),
        )(
            ids,
            *[toks[c] for c in group],
            *[cots[c] for c in group],
            *back[group],
            *[a for m, g in sums for a in (*m, *g)],
        )
        if last:
            mixed, token_grad, gate_grad = made
            break
        for i, c in enumerate(group):
            if c == 4:
                mixes[1], grads[-1] = along_z(made[0], -1), along_z(made[1], 1)
            else:
                sign = c // abs(c)
                mixes[sign] = along_z(made[2 * i], -sign)
                grads[sign] = along_z(made[2 * i + 1], -sign)

    grad_gate, grad_up = summed[0].astype(F32), summed[1].astype(F32)
    grad_down = jnp.swapaxes(summed[2], 1, 2).astype(F32)
    return mixed, token_grad, gate_grad.T, grad_gate, grad_up, grad_down


def solution(mesh):
    token_spec, row_spec, column_spec = (
        P(("expert", "fsdp"), None),
        P("expert", "fsdp", None),
        P("expert", None, "fsdp"),
    )
    return jax.shard_map(
        body,
        mesh=mesh,
        in_specs=(token_spec,) * 3 + (row_spec,) * 2 + (column_spec, token_spec),
        out_specs=(token_spec,) * 3 + (row_spec,) * 2 + (column_spec,),
        check_vma=False,
    )
```

```python
import jax
import jax.numpy as jnp
from jax import lax
from jax.experimental import pallas as pl
from jax.experimental.pallas import tpu as pltpu
from jax.sharding import PartitionSpec as P

NY, NZ, NF = 4, 8, 8
LOCAL = 2
D, FF, TOPK, TOK = 1024, 512, 8, 128
CAP = 20
META = 128
BF, F32 = jnp.bfloat16, jnp.float32
LIMIT = 56 * 1024 * 1024

GROUPS = ((0,), (1, -1), (2, -2), (3, -3), (4,))
SWAPPED = ()
WHOLE_OUT, WHOLE_BACK = False, False
WIDE = 2 * D + META


def rows_of(group):
    return -(-len(group) * CAP // 8) * 8


def nn(a, b):
    return lax.dot_general(a, b, (((1,), (0,)), ((), ())), preferred_element_type=F32)


def nt(a, b):
    return lax.dot_general(a, b, (((1,), (1,)), ((), ())), preferred_element_type=F32)


def tn(a, b):
    return lax.dot_general(a, b, (((0,), (0,)), ((), ())), preferred_element_type=F32)


def split3(v):
    hi = v.astype(BF)
    rest = v - hi.astype(F32)
    mid = rest.astype(BF)
    low = (rest - mid.astype(F32)).astype(BF)
    return [hi, mid, low]


def join3(block):
    return (block[0:8] + block[8:16]) + block[16:24]


def meta_block(routes, gates):
    parts = [routes.astype(F32)] + [p.astype(F32) for p in split3(gates)]
    parts.append(jnp.zeros((TOK - 32, META), F32))
    return jnp.concatenate(parts, axis=0)


def selection(ids, metas, depth):
    lanes = TOK * len(metas)
    blocks = [m.astype(F32) for m in metas]
    routes = jnp.concatenate([b[0:8] for b in blocks], axis=1)
    gates = jnp.concatenate([join3(b[8:32]) for b in blocks], axis=1)
    hits = [routes[k : k + 1, :] == ids for k in range(TOPK)]
    mask = jnp.zeros((8, lanes), F32)
    gate = jnp.zeros((8, lanes), F32)
    for k in range(TOPK):
        mask = mask + jnp.where(hits[k], 1.0, 0.0)
        gate = gate + jnp.where(hits[k], gates[k : k + 1, :], 0.0)
    above = lax.broadcasted_iota(jnp.int32, (lanes, lanes), 0)
    along = lax.broadcasted_iota(jnp.int32, (lanes, lanes), 1)
    earlier = (above < along) & (above // TOK == along // TOK)
    rank = nn(mask.astype(BF), jnp.where(earlier, 1.0, 0.0).astype(BF))
    chunk = lax.broadcasted_iota(jnp.int32, (8, lanes), 1) // TOK
    key = jnp.where(mask > 0.5, rank.astype(jnp.int32) + CAP * chunk, -1)
    place = lax.broadcasted_iota(jnp.int32, (8, depth, lanes), 1)
    pick = jnp.where(key[:, None, :] == place, 1.0, 0.0)
    row_gate = jnp.sum(pick * gate[:, None, :], axis=2, keepdims=True)
    return pick, row_gate, hits


def pack(ids, metas, feats, grads, depth, outs):
    pick, row_gate, _ = selection(ids, metas, depth)
    flat = pick.reshape(8 * depth, TOK * len(metas)).astype(BF)
    rows = nn(flat, jnp.concatenate(feats, axis=0)).reshape(8, depth, D)
    scaled = nn(flat, jnp.concatenate(grads, axis=0)).reshape(8, depth, D) * row_gate
    step = 8 // len(outs)
    for r, out in enumerate(outs):
        out[:, :, 0:D] = rows[step * r : step * (r + 1)].astype(BF)
        out[:, :, D:] = scaled[step * r : step * (r + 1)].astype(BF)


def first_kernel(ids_ref, tok_ref, cot_ref, routes_ref, gates_ref, *outs):
    meta = meta_block(routes_ref[...], gates_ref[...])
    wide_ref, outs = outs[0], outs[1:]
    wide_ref[:, 0:D] = tok_ref[...]
    if WHOLE_OUT:
        wide_ref[:, D : 2 * D] = cot_ref[...]
    wide_ref[:, wide_ref.shape[1] - META :] = meta.astype(BF)
    pack(ids_ref[:, 0:1], [meta[0:32]], [tok_ref[...]], [cot_ref[...]], rows_of((0,)), outs)


def chunk_views(refs):
    if WHOLE_OUT:
        metas = [r[0:32, 2 * D :] for r in refs]
        feats, cots = [r[:, 0:D] for r in refs], [r[:, D : 2 * D] for r in refs]
    else:
        metas = [r[0:32, D:] for r in refs[0::2]]
        feats, cots = [r[:, 0:D] for r in refs[0::2]], [r[...] for r in refs[1::2]]
    return metas, feats, cots


def held_refs(group):
    return len(group) * (1 if WHOLE_OUT else 2)


def pack_kernel(group, *refs):
    n = held_refs(group)
    pack(refs[0][:, 0:1], *chunk_views(refs[1 : n + 1]), rows_of(group), refs[n + 1 :])


def parts_of(group):
    return 1 if group in SWAPPED else NY


def expert_kernel(groups, *refs):
    n = sum(parts_of(g) for g in groups)
    ins, w_ref, outs = refs[:n], refs[n], refs[n + 1 : 2 * n + 1]
    rows_ref, hid_ref, gg_ref, ug_ref, stage = refs[2 * n + 1 :]
    spans, at, i = [], 0, 0
    for group in groups:
        depth = rows_of(group)
        for r in range(NY):
            place = (i, r) if group in SWAPPED else (i + r, 0)
            spans.append((*place, at, at + depth))
            at += depth
        i += parts_of(group)
    for i, r, lo, hi in spans:
        stage[lo:hi, :] = ins[i][r, 0].astype(F32)
    rows_ref[0] = stage[...].astype(BF)
    feats, grads = rows_ref[0, :, 0:D], rows_ref[0, :, D:]
    w_gate = w_ref[:, 0, 0].reshape(D, FF)
    w_up = w_ref[:, 1, 0].reshape(D, FF)
    w_down = w_ref[:, 2, 0].reshape(D, FF)
    gate_pre = nn(feats, w_gate)
    up_pre = nn(feats, w_up)
    sig = jax.nn.sigmoid(gate_pre)
    act = gate_pre * sig
    hidden = (act * up_pre).astype(BF)
    out = nt(hidden, w_down)
    for i, r, lo, hi in spans:
        outs[i][r, 0, :, 0:D] = out[lo:hi].astype(BF)
    hidden_grad = nn(grads, w_down)
    gate_grad = (hidden_grad * up_pre * sig * (1.0 + gate_pre * (1.0 - sig))).astype(BF)
    up_grad = (hidden_grad * act).astype(BF)
    back = nt(gate_grad, w_gate) + nt(up_grad, w_up)
    for i, r, lo, hi in spans:
        outs[i][r, 0, :, D:] = back[lo:hi].astype(BF)
    hid_ref[0], gg_ref[0], ug_ref[0] = hidden, gate_grad, up_grad


def weight_kernel(count, *refs):
    out_ref, refs = refs[-1], refs[:count]
    held = [jnp.concatenate([r[0] for r in refs[i::4]], axis=0) for i in range(4)]
    rows, hid, gate, up = held
    feats, grads = rows[:, 0:D], rows[:, D:]
    for i, (a, b) in enumerate(((feats, gate), (feats, up), (grads, hid))):
        out_ref[:, i, 0] = tn(a, b).astype(BF).reshape(NF, D // NF, FF)


def combine_kernel(group, *refs):
    count, depth = len(group), rows_of(group)
    lanes, n = TOK * count, held_refs(group)
    metas, _, cots = chunk_views(refs[1 : n + 1])
    backs = refs[n + 1 : n + 1 + parts_of(group)]
    outs = refs[n + 1 + parts_of(group) :]
    pick, row_gate, hits = selection(refs[0][:, 0:1], metas, depth)
    flat = pick.reshape(8 * depth, lanes).astype(BF)
    out = jnp.concatenate([r[:, :, 0:D].astype(F32) for r in backs], axis=0)
    back = jnp.concatenate([r[:, :, D:].astype(F32) for r in backs], axis=0)
    cot = nn(flat, jnp.concatenate(cots, axis=0)).reshape(8, depth, D)
    dots = jnp.sum(cot * out, axis=2, keepdims=True)
    by_expert = jnp.sum(pick * dots, axis=1)
    gate_grad = jnp.concatenate(
        [jnp.sum(jnp.where(h, by_expert, 0.0), axis=0, keepdims=True) for h in hits], axis=0
    )
    mixed = tn(flat, (out * row_gate).reshape(8 * depth, D).astype(BF))
    token = tn(flat, back.reshape(8 * depth, D).astype(BF))
    for i in range(count):
        span = slice(i * TOK, (i + 1) * TOK)
        parts = [p.astype(F32) for p in split3(gate_grad[:, span])]
        parts.append(jnp.zeros((TOK - 24, META), F32))
        meta = jnp.concatenate(parts, axis=0)
        if WHOLE_BACK:
            ref = outs[i]
            ref[:, 0:D] = mixed[span].astype(ref.dtype)
            ref[:, D : 2 * D] = token[span].astype(ref.dtype)
            ref[:, 2 * D :] = meta.astype(ref.dtype)
        else:
            mix_ref, tok_ref = outs[2 * i : 2 * i + 2]
            mix_ref[...] = mixed[span].astype(mix_ref.dtype)
            tok_ref[:, 0:D] = token[span].astype(tok_ref.dtype)
            tok_ref[:, D:] = meta.astype(tok_ref.dtype)


def shape(*dims, dtype=BF):
    return jax.ShapeDtypeStruct(dims, dtype)


def params(**kw):
    return pltpu.CompilerParams(vmem_limit_bytes=LIMIT, **kw)


def cost(flops, nbytes):
    return pl.CostEstimate(flops=1024, bytes_accessed=1024, transcendentals=0)


def along_z(a, step):
    pairs = [(y * NZ + z, y * NZ + (z + step) % NZ) for y in range(NY) for z in range(NZ)]
    return lax.ppermute(a, "expert", pairs)


def along_y(arrays, sign):
    if len(arrays) == 1:
        groups = [[y * NZ + z for y in range(NY)] for z in range(NZ)]
        return [
            lax.all_to_all(
                arrays[0], "expert", split_axis=0, concat_axis=0, axis_index_groups=groups, tiled=True
            )
        ]
    return [arrays[0]] + [
        lax.ppermute(
            arrays[r],
            "expert",
            [(y * NZ + z, (y + sign * r) % NY * NZ + z) for y in range(NY) for z in range(NZ)],
        )
        for r in range(1, NY)
    ]


def anywhere(count):
    return [pl.BlockSpec(memory_space=pl.ANY)] * count


def call(kernel, after, args, **kw):
    n = len(args)
    in_specs = kw.pop("in_specs", [pl.BlockSpec(memory_space=pltpu.VMEM)] * n) + anywhere(len(after))
    m = len(after)
    return pl.pallas_call(
        lambda *refs: kernel(*refs[:n], *refs[n + m :]),
        in_specs=in_specs,
        compiler_params=params(),
        **kw,
    )(*args, *after)


def row_shapes(group):
    n = parts_of(group)
    return [shape(8 // n, rows_of(group), 2 * D)] * n


def body(tokens, routes, gates, w_gate, w_up, w_down, cotangent):
    spot = lax.axis_index("expert")
    own = jnp.arange(2 * NY, dtype=jnp.int32)
    turned = LOCAL * ((spot // NZ + own // 2) % NY * NZ + spot % NZ) + own % 2
    straight = LOCAL * (own // 2 * NZ + spot % NZ) + own % 2
    turned, straight = (
        jnp.broadcast_to(i.astype(F32)[:, None], (8, 128)) for i in (turned, straight)
    )

    def ids(group):
        return straight if group in SWAPPED else turned

    shards = jnp.stack([w_gate, w_up, jnp.swapaxes(w_down, 1, 2)], axis=0)
    weights = lax.all_gather(shards, "fsdp", axis=0, tiled=False)

    first, arrived = (0,), {}
    wide, *packed = call(
        first_kernel,
        [],
        [ids(first), tokens, cotangent, routes.T, gates.T],
        out_shape=[shape(TOK, WIDE if WHOLE_OUT else D + META)] + row_shapes(first),
        name="first",
    )
    arrived[first] = along_y(packed, 1)
    held = {0: [wide] if WHOLE_OUT else [wide, cotangent]}
    for d in range(1, 4):
        for sign in (1, -1):
            held[sign * d] = [along_z(a, sign) for a in held[sign * (d - 1)]]
    if WHOLE_OUT:
        half = TOK // 2
        up, down = along_z(held[3][0][:half], 1), along_z(held[-3][0][half:], -1)
        held[4] = [jnp.concatenate([up, down], axis=0)]
    else:
        held[4] = [along_z(held[3][0], 1), along_z(held[-3][1], -1)]

    for g, group in list(enumerate(GROUPS))[1:]:
        before = arrived[GROUPS[max(g - 2, 0)]]
        packed = call(
            lambda *refs, group=group: pack_kernel(group, *refs),
            [packed[0], *(before[1:] or before)],
            [ids(group), *[a for c in group for a in held[c]]],
            out_shape=row_shapes(group),
            name="pack",
            cost_estimate=cost(2 * 8 * rows_of(group) * TOK * len(group) * 2 * D, 8 << 20),
        )
        arrived[group] = along_y(packed, 1)

    kept, returned, earlier = [], {}, [packed[0]]
    for part in (GROUPS[:3], GROUPS[3:]):
        rows = NY * sum(rows_of(g) for g in part)
        blocks, shapes, args = [], [], []
        for g in part:
            n = parts_of(g)
            blocks += [pl.BlockSpec((NY // n, 1, rows_of(g), 2 * D), lambda j: (0, j, 0, 0))] * n
            shapes += [shape(NY // n, 2, rows_of(g), 2 * D)] * n
            args += [a.reshape(NY // n, 2, rows_of(g), 2 * D) for a in arrived[g]]
        wide = pl.BlockSpec((1, rows, 2 * D), lambda j: (j, 0, 0))
        narrow = pl.BlockSpec((1, rows, FF), lambda j: (j, 0, 0))
        made = call(
            lambda *refs, part=part: expert_kernel(part, *refs),
            earlier,
            [*args, weights],
            grid=(LOCAL,),
            in_specs=blocks + [pl.BlockSpec((NF, 3, 1, D // NF, FF), lambda j: (0, 0, j, 0, 0))],
            out_specs=blocks + [wide] + [narrow] * 3,
            out_shape=shapes + [shape(2, rows, 2 * D)] + [shape(2, rows, FF)] * 3,
            scratch_shapes=[pltpu.VMEM((rows, 2 * D), F32)],
            name="expert",
            cost_estimate=cost(8e9, 16 << 20),
        )
        made = list(made)
        for g in part:
            n = parts_of(g)
            returned[g], made = [a.reshape(8 // n, rows_of(g), 2 * D) for a in made[:n]], made[n:]
        kept += made
        earlier = made[1:2]

    back = {g: along_y(returned[g], -1) for g in GROUPS[::-1]}

    coming = {1: [None, None], -1: [None, None]}
    earlier = []
    for group in GROUPS[::-1]:
        shapes = []
        for c in group:
            if WHOLE_BACK:
                shapes.append(shape(TOK, WIDE, dtype=BF if c == 4 else F32))
            else:
                shapes.append(shape(TOK, D, dtype=BF if c in (4, -3) else F32))
                shapes.append(shape(TOK, D + META, dtype=BF if c in (4, 3) else F32))
        made = call(
            lambda *refs, group=group: combine_kernel(group, *refs),
            earlier,
            [ids(group), *[a for c in group for a in held[c]], *back[group]],
            out_shape=shapes,
            name="combine",
            cost_estimate=cost(2 * 8 * rows_of(group) * TOK * len(group) * 3 * D, 12 << 20),
        )
        n = len(made) // len(group)
        earlier = [made[0]]
        if group == GROUPS[-1]:
            before = back[GROUPS[-2]]
            partial = call(
                lambda *refs: weight_kernel(len(kept), *refs),
                [made[0], *(before[1:] or before)],
                kept,
                grid=(LOCAL,),
                in_specs=[pl.BlockSpec((1,) + a.shape[1:], lambda j: (j, 0, 0)) for a in kept],
                out_specs=pl.BlockSpec((NF, 3, 1, D // NF, FF), lambda j: (0, 0, j, 0, 0)),
                out_shape=shape(NF, 3, LOCAL, D // NF, FF),
                name="weight_grads",
                cost_estimate=cost(10e9, 16 << 20),
            )
            summed = lax.psum_scatter(partial, "fsdp", scatter_dimension=0, tiled=False)
            earlier.append(partial)
        elif group != first:
            earlier += [a[0] if isinstance(a, tuple) else a for a in coming[1] + coming[-1] if a is not None]
        for i, c in enumerate(group):
            mine = made[i * n : (i + 1) * n]
            if c == 4 and WHOLE_BACK:
                half = TOK // 2
                up, down = along_z(mine[0][:half], -1), along_z(mine[0][half:], 1)
                coming[1], coming[-1] = [(up, 0)], [(down, half)]
            elif c == 4:
                coming[1], coming[-1] = [along_z(mine[0], -1), None], [None, along_z(mine[1], 1)]
            elif c != 0:
                sign = c // abs(c)
                coming[sign] = [
                    along_z(joined(a, came), -sign) for a, came in zip(mine, coming[sign])
                ]
    totals = [
        a + up.astype(F32) + down.astype(F32) for a, up, down in zip(mine, coming[1], coming[-1])
    ]
    if WHOLE_BACK:
        (total,) = totals
        mixed, token_grad = total[:, 0:D], total[:, D : 2 * D]
    else:
        mixed, total = totals
        token_grad = total[:, 0:D]
    gate_grad = join3(total[0:24, total.shape[1] - META :]).T
    grad_gate, grad_up = summed[0].astype(F32), summed[1].astype(F32)
    grad_down = jnp.swapaxes(summed[2], 1, 2).astype(F32)
    return mixed.astype(BF), token_grad.astype(BF), gate_grad, grad_gate, grad_up, grad_down


def joined(own, came):
    if came is None:
        return own.astype(BF)
    if isinstance(came, tuple):
        came, at = came
        half = came.shape[0]
        added = own[at : at + half] + came.astype(F32)
        parts = [added, own[half:]] if at == 0 else [own[:at], added]
        return jnp.concatenate(parts, axis=0).astype(BF)
    return (own + came.astype(F32)).astype(BF)


def solution(mesh):
    token_spec, row_spec, column_spec = (
        P(("expert", "fsdp"), None),
        P("expert", "fsdp", None),
        P("expert", None, "fsdp"),
    )
    return jax.shard_map(
        body,
        mesh=mesh,
        in_specs=(token_spec,) * 3 + (row_spec,) * 2 + (column_spec, token_spec),
        out_specs=(token_spec,) * 3 + (row_spec,) * 2 + (column_spec,),
        check_vma=False,
    )
```

```python
import jax
import jax.numpy as jnp
from jax import lax
from jax.experimental import pallas as pl
from jax.experimental.pallas import tpu as pltpu
from jax.sharding import PartitionSpec as P

NY, NZ, NF = 4, 8, 8
LOCAL = 2
D, FF, TOPK, TOK = 1024, 512, 8, 128
CAP = 20
META = 128
BF, F32 = jnp.bfloat16, jnp.float32
LIMIT = 56 * 1024 * 1024

GROUPS = ((1, -1), (2, -2), (3, -3), (0, 4))
SWAPPED = ()
WHOLE_OUT, WHOLE_BACK = False, False
WIDE = 2 * D + META


def rows_of(group):
    return -(-len(group) * CAP // 8) * 8


def nn(a, b):
    return lax.dot_general(a, b, (((1,), (0,)), ((), ())), preferred_element_type=F32)


def nt(a, b):
    return lax.dot_general(a, b, (((1,), (1,)), ((), ())), preferred_element_type=F32)


def tn(a, b):
    return lax.dot_general(a, b, (((0,), (0,)), ((), ())), preferred_element_type=F32)


def split3(v):
    hi = v.astype(BF)
    rest = v - hi.astype(F32)
    mid = rest.astype(BF)
    low = (rest - mid.astype(F32)).astype(BF)
    return [hi, mid, low]


def join3(block):
    return (block[0:8] + block[8:16]) + block[16:24]


def meta_block(routes, gates):
    parts = [routes.astype(F32)] + [p.astype(F32) for p in split3(gates)]
    parts.append(jnp.zeros((TOK - 32, META), F32))
    return jnp.concatenate(parts, axis=0)


def selection(ids, metas, depth):
    lanes = TOK * len(metas)
    blocks = [m.astype(F32) for m in metas]
    routes = jnp.concatenate([b[0:8] for b in blocks], axis=1)
    gates = jnp.concatenate([join3(b[8:32]) for b in blocks], axis=1)
    hits = [routes[k : k + 1, :] == ids for k in range(TOPK)]
    mask = jnp.zeros((8, lanes), F32)
    gate = jnp.zeros((8, lanes), F32)
    for k in range(TOPK):
        mask = mask + jnp.where(hits[k], 1.0, 0.0)
        gate = gate + jnp.where(hits[k], gates[k : k + 1, :], 0.0)
    above = lax.broadcasted_iota(jnp.int32, (lanes, lanes), 0)
    along = lax.broadcasted_iota(jnp.int32, (lanes, lanes), 1)
    earlier = (above < along) & (above // TOK == along // TOK)
    rank = nn(mask.astype(BF), jnp.where(earlier, 1.0, 0.0).astype(BF))
    chunk = lax.broadcasted_iota(jnp.int32, (8, lanes), 1) // TOK
    key = jnp.where(mask > 0.5, rank.astype(jnp.int32) + CAP * chunk, -1)
    place = lax.broadcasted_iota(jnp.int32, (8, depth, lanes), 1)
    pick = jnp.where(key[:, None, :] == place, 1.0, 0.0)
    row_gate = jnp.sum(pick * gate[:, None, :], axis=2, keepdims=True)
    return pick, row_gate, hits


def pack(ids, metas, feats, grads, depth, outs):
    pick, row_gate, _ = selection(ids, metas, depth)
    flat = pick.reshape(8 * depth, TOK * len(metas)).astype(BF)
    rows = nn(flat, jnp.concatenate(feats, axis=0)).reshape(8, depth, D)
    scaled = nn(flat, jnp.concatenate(grads, axis=0)).reshape(8, depth, D) * row_gate
    step = 8 // len(outs)
    for r, out in enumerate(outs):
        out[:, :, 0:D] = rows[step * r : step * (r + 1)].astype(BF)
        out[:, :, D:] = scaled[step * r : step * (r + 1)].astype(BF)


def first_kernel(tok_ref, cot_ref, routes_ref, gates_ref, wide_ref):
    wide_ref[:, 0:D] = tok_ref[...]
    if WHOLE_OUT:
        wide_ref[:, D : 2 * D] = cot_ref[...]
    wide_ref[:, wide_ref.shape[1] - META :] = meta_block(routes_ref[...], gates_ref[...]).astype(BF)


def chunk_views(refs):
    if WHOLE_OUT:
        metas = [r[0:32, 2 * D :] for r in refs]
        feats, cots = [r[:, 0:D] for r in refs], [r[:, D : 2 * D] for r in refs]
    else:
        metas = [r[0:32, D:] for r in refs[0::2]]
        feats, cots = [r[:, 0:D] for r in refs[0::2]], [r[...] for r in refs[1::2]]
    return metas, feats, cots


def held_refs(group):
    return len(group) * (1 if WHOLE_OUT else 2)


def pack_kernel(group, *refs):
    n = held_refs(group)
    pack(refs[0][:, 0:1], *chunk_views(refs[1 : n + 1]), rows_of(group), refs[n + 1 :])


def parts_of(group):
    return 1 if group in SWAPPED else NY


def expert_kernel(groups, *refs):
    n = sum(parts_of(g) for g in groups)
    ins, w_ref, outs = refs[:n], refs[n], refs[n + 1 : 2 * n + 1]
    rows_ref, hid_ref, gg_ref, ug_ref, stage = refs[2 * n + 1 :]
    spans, at, i = [], 0, 0
    for group in groups:
        depth = rows_of(group)
        for r in range(NY):
            place = (i, r) if group in SWAPPED else (i + r, 0)
            spans.append((*place, at, at + depth))
            at += depth
        i += parts_of(group)
    for i, r, lo, hi in spans:
        stage[lo:hi, :] = ins[i][r, 0].astype(F32)
    rows_ref[0] = stage[...].astype(BF)
    feats, grads = rows_ref[0, :, 0:D], rows_ref[0, :, D:]
    w_gate = w_ref[:, 0, 0].reshape(D, FF)
    w_up = w_ref[:, 1, 0].reshape(D, FF)
    w_down = w_ref[:, 2, 0].reshape(D, FF)
    gate_pre = nn(feats, w_gate)
    up_pre = nn(feats, w_up)
    sig = jax.nn.sigmoid(gate_pre)
    act = gate_pre * sig
    hidden = (act * up_pre).astype(BF)
    out = nt(hidden, w_down)
    for i, r, lo, hi in spans:
        outs[i][r, 0, :, 0:D] = out[lo:hi].astype(BF)
    hidden_grad = nn(grads, w_down)
    gate_grad = (hidden_grad * up_pre * sig * (1.0 + gate_pre * (1.0 - sig))).astype(BF)
    up_grad = (hidden_grad * act).astype(BF)
    back = nt(gate_grad, w_gate) + nt(up_grad, w_up)
    for i, r, lo, hi in spans:
        outs[i][r, 0, :, D:] = back[lo:hi].astype(BF)
    hid_ref[0], gg_ref[0], ug_ref[0] = hidden, gate_grad, up_grad


def weight_kernel(count, *refs):
    out_ref, refs = refs[-1], refs[:count]
    held = [jnp.concatenate([r[0] for r in refs[i::4]], axis=0) for i in range(4)]
    rows, hid, gate, up = held
    feats, grads = rows[:, 0:D], rows[:, D:]
    for i, (a, b) in enumerate(((feats, gate), (feats, up), (grads, hid))):
        out_ref[:, i, 0] = tn(a, b).astype(BF).reshape(NF, D // NF, FF)


def combine_kernel(group, *refs):
    count, depth = len(group), rows_of(group)
    lanes, n = TOK * count, held_refs(group)
    metas, _, cots = chunk_views(refs[1 : n + 1])
    backs = refs[n + 1 : n + 1 + parts_of(group)]
    outs = refs[n + 1 + parts_of(group) :]
    pick, row_gate, hits = selection(refs[0][:, 0:1], metas, depth)
    flat = pick.reshape(8 * depth, lanes).astype(BF)
    out = jnp.concatenate([r[:, :, 0:D].astype(F32) for r in backs], axis=0)
    back = jnp.concatenate([r[:, :, D:].astype(F32) for r in backs], axis=0)
    cot = nn(flat, jnp.concatenate(cots, axis=0)).reshape(8, depth, D)
    dots = jnp.sum(cot * out, axis=2, keepdims=True)
    by_expert = jnp.sum(pick * dots, axis=1)
    gate_grad = jnp.concatenate(
        [jnp.sum(jnp.where(h, by_expert, 0.0), axis=0, keepdims=True) for h in hits], axis=0
    )
    mixed = tn(flat, (out * row_gate).reshape(8 * depth, D).astype(BF))
    token = tn(flat, back.reshape(8 * depth, D).astype(BF))
    for i in range(count):
        span = slice(i * TOK, (i + 1) * TOK)
        parts = [p.astype(F32) for p in split3(gate_grad[:, span])]
        parts.append(jnp.zeros((TOK - 24, META), F32))
        meta = jnp.concatenate(parts, axis=0)
        if WHOLE_BACK:
            ref = outs[i]
            ref[:, 0:D] = mixed[span].astype(ref.dtype)
            ref[:, D : 2 * D] = token[span].astype(ref.dtype)
            ref[:, 2 * D :] = meta.astype(ref.dtype)
        else:
            mix_ref, tok_ref = outs[2 * i : 2 * i + 2]
            mix_ref[...] = mixed[span].astype(mix_ref.dtype)
            tok_ref[:, 0:D] = token[span].astype(tok_ref.dtype)
            tok_ref[:, D:] = meta.astype(tok_ref.dtype)


def shape(*dims, dtype=BF):
    return jax.ShapeDtypeStruct(dims, dtype)


def params(**kw):
    return pltpu.CompilerParams(vmem_limit_bytes=LIMIT, **kw)


def cost(flops, nbytes):
    return pl.CostEstimate(flops=1024, bytes_accessed=1024, transcendentals=0)


def along_z(a, step):
    pairs = [(y * NZ + z, y * NZ + (z + step) % NZ) for y in range(NY) for z in range(NZ)]
    return lax.ppermute(a, "expert", pairs)


def along_y(arrays, sign):
    if len(arrays) == 1:
        groups = [[y * NZ + z for y in range(NY)] for z in range(NZ)]
        return [
            lax.all_to_all(
                arrays[0], "expert", split_axis=0, concat_axis=0, axis_index_groups=groups, tiled=True
            )
        ]
    return [arrays[0]] + [
        lax.ppermute(
            arrays[r],
            "expert",
            [(y * NZ + z, (y + sign * r) % NY * NZ + z) for y in range(NY) for z in range(NZ)],
        )
        for r in range(1, NY)
    ]


def anywhere(count):
    return [pl.BlockSpec(memory_space=pl.ANY)] * count


def call(kernel, after, args, **kw):
    n = len(args)
    in_specs = kw.pop("in_specs", [pl.BlockSpec(memory_space=pltpu.VMEM)] * n) + anywhere(len(after))
    m = len(after)
    return pl.pallas_call(
        lambda *refs: kernel(*refs[:n], *refs[n + m :]),
        in_specs=in_specs,
        compiler_params=params(),
        **kw,
    )(*args, *after)


def row_shapes(group):
    n = parts_of(group)
    return [shape(8 // n, rows_of(group), 2 * D)] * n


def body(tokens, routes, gates, w_gate, w_up, w_down, cotangent):
    spot = lax.axis_index("expert")
    own = jnp.arange(2 * NY, dtype=jnp.int32)
    turned = LOCAL * ((spot // NZ + own // 2) % NY * NZ + spot % NZ) + own % 2
    straight = LOCAL * (own // 2 * NZ + spot % NZ) + own % 2
    turned, straight = (
        jnp.broadcast_to(i.astype(F32)[:, None], (8, 128)) for i in (turned, straight)
    )

    def ids(group):
        return straight if group in SWAPPED else turned

    shards = jnp.stack([w_gate, w_up, jnp.swapaxes(w_down, 1, 2)], axis=0)
    weights = lax.all_gather(shards, "fsdp", axis=0, tiled=False)

    (wide,) = call(
        first_kernel,
        [],
        [tokens, cotangent, routes.T, gates.T],
        out_shape=[shape(TOK, WIDE if WHOLE_OUT else D + META)],
        name="first",
    )
    arrived, packed = {}, []
    held = {0: [wide] if WHOLE_OUT else [wide, cotangent]}
    for d in range(1, 4):
        for sign in (1, -1):
            held[sign * d] = [along_z(a, sign) for a in held[sign * (d - 1)]]
    if WHOLE_OUT:
        half = TOK // 2
        up, down = along_z(held[3][0][:half], 1), along_z(held[-3][0][half:], -1)
        held[4] = [jnp.concatenate([up, down], axis=0)]
    else:
        held[4] = [along_z(held[3][0], 1), along_z(held[-3][1], -1)]

    for g, group in enumerate(GROUPS):
        before = arrived[GROUPS[g - 2]] if g > 1 else []
        packed = call(
            lambda *refs, group=group: pack_kernel(group, *refs),
            [*packed[:1], *(before[1:] or before)],
            [ids(group), *[a for c in group for a in held[c]]],
            out_shape=row_shapes(group),
            name="pack",
            cost_estimate=cost(2 * 8 * rows_of(group) * TOK * len(group) * 2 * D, 8 << 20),
        )
        arrived[group] = along_y(packed, 1)

    kept, returned, earlier = [], {}, [packed[0]]
    for part in (GROUPS[:2], GROUPS[2:]):
        rows = NY * sum(rows_of(g) for g in part)
        blocks, shapes, args = [], [], []
        for g in part:
            n = parts_of(g)
            blocks += [pl.BlockSpec((NY // n, 1, rows_of(g), 2 * D), lambda j: (0, j, 0, 0))] * n
            shapes += [shape(NY // n, 2, rows_of(g), 2 * D)] * n
            args += [a.reshape(NY // n, 2, rows_of(g), 2 * D) for a in arrived[g]]
        wide = pl.BlockSpec((1, rows, 2 * D), lambda j: (j, 0, 0))
        narrow = pl.BlockSpec((1, rows, FF), lambda j: (j, 0, 0))
        made = call(
            lambda *refs, part=part: expert_kernel(part, *refs),
            earlier,
            [*args, weights],
            grid=(LOCAL,),
            in_specs=blocks + [pl.BlockSpec((NF, 3, 1, D // NF, FF), lambda j: (0, 0, j, 0, 0))],
            out_specs=blocks + [wide] + [narrow] * 3,
            out_shape=shapes + [shape(2, rows, 2 * D)] + [shape(2, rows, FF)] * 3,
            scratch_shapes=[pltpu.VMEM((rows, 2 * D), F32)],
            name="expert",
            cost_estimate=cost(8e9, 16 << 20),
        )
        made = list(made)
        for g in part:
            n = parts_of(g)
            returned[g], made = [a.reshape(8 // n, rows_of(g), 2 * D) for a in made[:n]], made[n:]
        kept += made
        earlier = made[1:2]

    back = {g: along_y(returned[g], -1) for g in GROUPS[::-1]}

    coming = {1: [None, None], -1: [None, None]}
    earlier = []
    for group in GROUPS[::-1]:
        shapes = []
        for c in group:
            if WHOLE_BACK:
                shapes.append(shape(TOK, WIDE, dtype=BF if c == 4 else F32))
            else:
                shapes.append(shape(TOK, D, dtype=BF if c in (4, -3) else F32))
                shapes.append(shape(TOK, D + META, dtype=BF if c in (4, 3) else F32))
        made = call(
            lambda *refs, group=group: combine_kernel(group, *refs),
            earlier,
            [ids(group), *[a for c in group for a in held[c]], *back[group]],
            out_shape=shapes,
            name="combine",
            cost_estimate=cost(2 * 8 * rows_of(group) * TOK * len(group) * 3 * D, 12 << 20),
        )
        n = len(made) // len(group)
        earlier = [made[0]]
        if group == GROUPS[-1]:
            before = back[GROUPS[-2]]
            partial = call(
                lambda *refs: weight_kernel(len(kept), *refs),
                [made[0], *(before[1:] or before)],
                kept,
                grid=(LOCAL,),
                in_specs=[pl.BlockSpec((1,) + a.shape[1:], lambda j: (j, 0, 0)) for a in kept],
                out_specs=pl.BlockSpec((NF, 3, 1, D // NF, FF), lambda j: (0, 0, j, 0, 0)),
                out_shape=shape(NF, 3, LOCAL, D // NF, FF),
                name="weight_grads",
                cost_estimate=cost(10e9, 16 << 20),
            )
            summed = lax.psum_scatter(partial, "fsdp", scatter_dimension=0, tiled=False)
            earlier.append(partial)
        else:
            earlier += [a[0] if isinstance(a, tuple) else a for a in coming[1] + coming[-1] if a is not None]
        for i, c in enumerate(group):
            mine = made[i * n : (i + 1) * n]
            if c == 0:
                last = mine
            elif c == 4 and WHOLE_BACK:
                half = TOK // 2
                up, down = along_z(mine[0][:half], -1), along_z(mine[0][half:], 1)
                coming[1], coming[-1] = [(up, 0)], [(down, half)]
            elif c == 4:
                coming[1], coming[-1] = [along_z(mine[0], -1), None], [None, along_z(mine[1], 1)]
            else:
                sign = c // abs(c)
                coming[sign] = [
                    along_z(joined(a, came), -sign) for a, came in zip(mine, coming[sign])
                ]
    totals = [
        a + up.astype(F32) + down.astype(F32) for a, up, down in zip(last, coming[1], coming[-1])
    ]
    if WHOLE_BACK:
        (total,) = totals
        mixed, token_grad = total[:, 0:D], total[:, D : 2 * D]
    else:
        mixed, total = totals
        token_grad = total[:, 0:D]
    gate_grad = join3(total[0:24, total.shape[1] - META :]).T
    grad_gate, grad_up = summed[0].astype(F32), summed[1].astype(F32)
    grad_down = jnp.swapaxes(summed[2], 1, 2).astype(F32)
    return mixed.astype(BF), token_grad.astype(BF), gate_grad, grad_gate, grad_up, grad_down


def joined(own, came):
    if came is None:
        return own.astype(BF)
    if isinstance(came, tuple):
        came, at = came
        half = came.shape[0]
        added = own[at : at + half] + came.astype(F32)
        parts = [added, own[half:]] if at == 0 else [own[:at], added]
        return jnp.concatenate(parts, axis=0).astype(BF)
    return (own + came.astype(F32)).astype(BF)


def solution(mesh):
    token_spec, row_spec, column_spec = (
        P(("expert", "fsdp"), None),
        P("expert", "fsdp", None),
        P("expert", None, "fsdp"),
    )
    return jax.shard_map(
        body,
        mesh=mesh,
        in_specs=(token_spec,) * 3 + (row_spec,) * 2 + (column_spec, token_spec),
        out_specs=(token_spec,) * 3 + (row_spec,) * 2 + (column_spec,),
        check_vma=False,
    )
```
